128 devices in a mesh: grp: 4 (over y_lo, core), col: 32 (over y_hi, x, z).
Axes of the slice: x: 4, y: 4 (y_hi: 2, y_lo: 2; y = y_hi * 2 + y_lo), z: 4, core: 2. Of those that a mesh axis runs over, the one named last changes fastest.
Arguments:
- interferogram: float32 [512, 512, 2048], P('grp', 'col'), may hold values from -6 to 6
- sideband_start: int32 [1], replicated, may hold values from 1 to 767
- crop_start: int32 [2], replicated, may hold values from 0 to 384
Outputs:
- focal_field: float32 [2, 256, 128, 128], P(None, ('grp', 'col'))
The draws below stay inside these ranges and needn't reach their ends.
All inputs are finite; a program needn't handle non-finite values.
Results may differ from the reference program's by a relative error of at most 0.00007.
Values sent between devices are 32-bit elements; how exact they have to be, the bound alone decides.
No kernel may reach another device: no remote copies, remote signals or barrier semaphores. Data moves between devices by JAX's collectives and lax.ppermute only.
A program may use at most 128 MiB of HBM per device.

```python
import jax
import jax.numpy as jnp
from jax import lax

NR = 512
NC = 512
NT = 2048
NB = 256
CROP = 128


def block_scale(own_key, dims, pieces, least, top_value):
    def one(axis_at, parts):
        heights = jax.random.uniform(jax.random.fold_in(jax.random.fold_in(own_key, 6), axis_at), (parts,), jnp.float32, least / len(pieces), top_value / len(pieces))
        return jnp.repeat(jnp.exp(heights), dims[axis_at] // parts).reshape((-1,) + (1,) * (len(dims) - axis_at - 1))

    gain = one(*pieces[0])
    for cut in pieces[1:]:
        gain = gain * one(*cut)
    return gain


def centred(rng, shape, spread, reach, shards=(), held_as=jnp.bfloat16):
    drawn = jax.random.normal(rng, shape, jnp.float32) * spread
    if len(shards) > 0:
        drawn = block_scale(rng, shape, shards, -0.22, 0.18) * drawn
    return jnp.clip(drawn, min=-reach, max=reach).astype(held_as)


def setup_inputs(seed: int = 0) -> dict:
    seeds = jax.random.split(jax.random.key(seed), 4)
    interferogram = centred(seeds[0], (NR, NC, NT), 1.0, 6.0, ((0, 4), (1, 32)), jnp.float32)
    sideband_start = jax.random.randint(seeds[1], (1,), 1, NT // 2 - NB).astype(jnp.int32)
    crop_start = jax.random.randint(seeds[2], (2,), 0, min(NR, NC) - CROP + 1).astype(jnp.int32)
    return {"interferogram": interferogram, "sideband_start": sideband_start, "crop_start": crop_start}


def reference(interferogram, sideband_start, crop_start):
    start = sideband_start[0].astype(jnp.int32)
    blocks = interferogram.reshape(NR // 8, 8, NC, NT)

    def one_block(block):
        spectra = jnp.fft.fft(block, axis=-1, norm="ortho")
        return lax.dynamic_slice_in_dim(spectra, start, NB, 2)

    spectrum = lax.map(one_block, blocks).reshape(NR, NC, NB)
    focal = jnp.fft.fft2(spectrum, axes=(0, 1), norm="ortho")
    focal = lax.dynamic_slice_in_dim(focal, crop_start[0].astype(jnp.int32), CROP, 0)
    focal = lax.dynamic_slice_in_dim(focal, crop_start[1].astype(jnp.int32), CROP, 1)
    focal = jnp.transpose(focal, (2, 0, 1))
    return jnp.stack([jnp.real(focal), jnp.imag(focal)]).astype(jnp.float32)
```

```python
import functools
import math

import jax
import jax.numpy as jnp
from jax import lax
from jax.experimental import pallas as pl
from jax.experimental.pallas import tpu as pltpu
from jax.sharding import PartitionSpec as P

NR = 512
NC = 512
NT = 2048
NB = 256
CROP = 128
HALF = NT // 2
TURN = 2048
F32 = jnp.float32
BF16 = jnp.bfloat16


def cos_sin(u):
    v = u + 256
    quadrant = (v >> 9) & 3
    r = ((v & 511) - 256).astype(F32) * (2.0 * math.pi / TURN)
    z = r * r
    s = r + r * z * (-1.6666654611e-1 + z * (8.3321608736e-3 + z * -1.9515295891e-4))
    c = 1.0 - 0.5 * z + z * z * (4.166664568298827e-2 + z * (-1.388731625493765e-3 + z * 2.443315711809948e-5))
    odd = (quadrant & 1) == 1
    cos = jnp.where(odd, s, c)
    sin = jnp.where(odd, c, s)
    cos = jnp.where((quadrant == 1) | (quadrant == 2), -cos, cos)
    sin = jnp.where(quadrant >= 2, -sin, sin)
    return cos, sin


def split(a):
    hi = a.astype(BF16)
    return hi, (a - hi.astype(F32)).astype(BF16)


def dot(a, b, dims):
    return lax.dot_general(a, b, (dims, ((), ())), preferred_element_type=F32)


def dot3(a, b, dims):
    return dot(a[0], b[0], dims) + (dot(a[0], b[1], dims) + dot(a[1], b[0], dims))


NT_DIMS = ((1,), (1,))
NN_DIMS = ((1,), (0,))
TN_DIMS = ((0,), (0,))


def spectrum_kernel(scal, x_hbm, send_ref, keep_ref, xbuf, tab_hi, tab_lo, row_hi, row_lo, sums, sem):
    start, crop, core, row0 = scal[0], scal[1], scal[2], scal[3]
    copies = []
    for h in range(2):
        for tt in range(16):
            cp = pltpu.make_async_copy(
                x_hbm.at[:, pl.ds(8 * h, 8), pl.ds(128 * tt, 128)], xbuf.at[h, tt], sem.at[h, tt]
            )
            cp.start()
            copies.append(cp)

    scale = 1.0 / math.sqrt(NT)

    def one_table(i, _):
        e = i >> 3
        m = (i & 7) * 16 + lax.broadcasted_iota(jnp.int32, (16, HALF), 0)
        t = lax.broadcasted_iota(jnp.int32, (16, HALF), 1)
        owner = jnp.where(m < 64, 1 - core, core)
        j = (m & 32) * 2 + owner * 32 + (m & 31)
        cos, sin = cos_sin(((start + 2 * j + e) * t) & (TURN - 1))
        for part, val in ((0, cos * scale), (1, sin * -scale)):
            hi, lo = split(val)
            rows = pl.ds(pl.multiple_of(e * 256 + part * 128 + (i & 7) * 16, 16), 16)
            tab_hi[rows, :] = hi
            tab_lo[rows, :] = lo
        return 0

    lax.fori_loop(0, 16, one_table, 0)

    rscale = 1.0 / math.sqrt(NR)
    r = row0 + lax.broadcasted_iota(jnp.int32, (128, CROP), 0)
    p = crop + lax.broadcasted_iota(jnp.int32, (128, CROP), 1)
    cos, sin = cos_sin(((r * p) & (NR - 1)) * (TURN // NR))
    cos, sin = cos * rscale, sin * rscale
    for rows, cols, val in ((0, 0, cos), (0, 128, -sin), (128, 0, sin), (128, 128, cos)):
        hi, lo = split(val)
        row_hi[rows : rows + 128, cols : cols + 128] = hi
        row_lo[rows : rows + 128, cols : cols + 128] = lo

    sign = jnp.where((start & 1) == 0, 1.0, -1.0).astype(F32)

    for h in range(2):
        for tt in range(16):
            copies[16 * h + tt].wait()
        xr = xbuf.at[h].reshape(16, 1024, 128)

        def pair(i, _):
            parts = [[], []]
            for cc in range(2):
                rows = pl.ds(2 * i + cc, 128, stride=8)
                a = [xr[tt, rows, :] for tt in range(8)]
                b = [xr[8 + tt, rows, :] * sign for tt in range(8)]
                parts[0].append(jnp.concatenate([v + w for v, w in zip(a, b)], axis=1))
                parts[1].append(jnp.concatenate([v - w for v, w in zip(a, b)], axis=1))
            for e in range(2):
                y = split(jnp.concatenate(parts[e], axis=0))
                d = dot3(
                    (tab_hi[256 * e : 256 * e + 256, :], tab_lo[256 * e : 256 * e + 256, :]), y, NT_DIMS
                )
                for cc in range(2):
                    rows = pl.ds(pl.multiple_of((e * 8 + 2 * i + cc) * 128, 128), 128)
                    sums[rows, 0:128] = d[0:128, 128 * cc : 128 * cc + 128]
                    sums[rows, 128:256] = d[128:256, 128 * cc : 128 * cc + 128]
            return 0

        lax.fori_loop(0, 4, pair, 0)

        def rowwise(i, _):
            rows = pl.ds(pl.multiple_of(i * 512, 512), 512)
            g = dot3(split(sums[rows, :]), (row_hi[...], row_lo[...]), NN_DIMS)
            for k in range(4):
                ec = i * 4 + k
                first = (ec // 8) * 32 + 8 * h + ec % 8
                for rel, ref in ((0, send_ref), (1, keep_ref)):
                    for y in range(2):
                        at = k * 128 + rel * 64 + y * 32
                        for ri in range(2):
                            ref[pl.ds(y * 64 + ri * 16 + first, 32, stride=128), :] = g[
                                at : at + 32, 128 * ri : 128 * ri + 128
                            ]
            return 0

        lax.fori_loop(0, 4, rowwise, 0)


def spectrum_call(scal, x):
    out = jax.ShapeDtypeStruct((4096, 128), F32)
    return pl.pallas_call(
        spectrum_kernel,
        out_shape=(out, out),
        in_specs=[pl.BlockSpec(memory_space=pltpu.SMEM), pl.BlockSpec(memory_space=pl.ANY)],
        out_specs=(pl.BlockSpec(memory_space=pltpu.VMEM), pl.BlockSpec(memory_space=pltpu.VMEM)),
        scratch_shapes=[
            pltpu.VMEM((2, 16, 128, 8, 128), F32),
            pltpu.VMEM((512, HALF), BF16),
            pltpu.VMEM((512, HALF), BF16),
            pltpu.VMEM((256, 256), BF16),
            pltpu.VMEM((256, 256), BF16),
            pltpu.VMEM((2048, 256), F32),
            pltpu.SemaphoreType.DMA((2, 16)),
        ],
        compiler_params=pltpu.CompilerParams(vmem_limit_bytes=48 * 2**20),
        name="spectrum",
    )(scal, x)


def focal_kernel(scal, g_ref, send_ref, keep_ref, tab_hi, tab_lo):
    crop, mine = scal[0], scal[1]
    scale = 1.0 / math.sqrt(NC)
    c = lax.broadcasted_iota(jnp.int32, (NC, CROP), 0)
    q = crop + lax.broadcasted_iota(jnp.int32, (NC, CROP), 1)
    cos, sin = cos_sin(((c * q) & (NC - 1)) * (TURN // NC))
    for lane, val in ((0, cos * scale), (128, sin * scale)):
        hi, lo = split(val)
        tab_hi[:, lane : lane + 128] = hi
        tab_lo[:, lane : lane + 128] = lo
    for rel, ref in ((0, send_ref), (1, keep_ref)):
        y = 1 - mine if rel == 0 else mine
        for e in range(2):
            g = [g_ref[:, y, e, ri, :, :].reshape(NC, CROP) for ri in range(2)]
            g = jnp.concatenate(g, axis=1)
            u = dot3(split(g), (tab_hi[...], tab_lo[...]), TN_DIMS)
            ref[0, e] = u[0:128, 0:128] + u[128:256, 128:256]
            ref[1, e] = u[128:256, 0:128] - u[0:128, 128:256]


def focal_call(scal, g):
    out = jax.ShapeDtypeStruct((2, 2, CROP, CROP), F32)
    return pl.pallas_call(
        focal_kernel,
        out_shape=(out, out),
        in_specs=[pl.BlockSpec(memory_space=pltpu.SMEM), pl.BlockSpec(memory_space=pltpu.VMEM)],
        out_specs=(pl.BlockSpec(memory_space=pltpu.VMEM), pl.BlockSpec(memory_space=pltpu.VMEM)),
        scratch_shapes=[pltpu.VMEM((NC, 256), BF16), pltpu.VMEM((NC, 256), BF16)],
        compiler_params=pltpu.CompilerParams(vmem_limit_bytes=24 * 2**20),
        name="focal",
    )(scal, g)


def on_device(interferogram, sideband_start, crop_start):
    grp = lax.axis_index("grp")
    core, y_lo = grp & 1, grp >> 1
    scal = jnp.stack([sideband_start[0], crop_start[0], core, grp * 128]).astype(jnp.int32)
    send, keep = spectrum_call(scal, interferogram)
    got = lax.ppermute(send, "grp", [(i, i ^ 1) for i in range(4)])
    mine = (keep + got).reshape(32, 128, 128)
    gathered = lax.all_to_all(mine, "col", split_axis=0, concat_axis=0, tiled=True)
    scal = jnp.stack([crop_start[1], y_lo]).astype(jnp.int32)
    send, keep = focal_call(scal, gathered.reshape(32, 2, 2, 2, 16, 128))
    got = lax.ppermute(send, "grp", [(i, i ^ 2) for i in range(4)])
    return keep + got


def solution(mesh):
    return jax.shard_map(
        on_device,
        mesh=mesh,
        in_specs=(P("grp", "col", None), P(), P()),
        out_specs=P(None, ("grp", "col"), None, None),
        check_vma=False,
    )
```

```python
import functools
import math

import jax
import jax.numpy as jnp
from jax import lax
from jax.experimental import pallas as pl
from jax.experimental.pallas import tpu as pltpu
from jax.sharding import PartitionSpec as P

NR = 512
NC = 512
NT = 2048
NB = 256
CROP = 128
HALF = NT // 2
TURN = 2048
F32 = jnp.float32
BF16 = jnp.bfloat16


def cos_sin(u):
    v = u + 256
    quadrant = (v >> 9) & 3
    r = ((v & 511) - 256).astype(F32) * (2.0 * math.pi / TURN)
    z = r * r
    s = r + r * z * (-1.6666654611e-1 + z * (8.3321608736e-3 + z * -1.9515295891e-4))
    c = 1.0 - 0.5 * z + z * z * (4.166664568298827e-2 + z * (-1.388731625493765e-3 + z * 2.443315711809948e-5))
    odd = (quadrant & 1) == 1
    cos = jnp.where(odd, s, c)
    sin = jnp.where(odd, c, s)
    cos = jnp.where((quadrant == 1) | (quadrant == 2), -cos, cos)
    sin = jnp.where(quadrant >= 2, -sin, sin)
    return cos, sin


def split(a):
    hi = a.astype(BF16)
    return hi, (a - hi.astype(F32)).astype(BF16)


def dot(a, b, dims):
    return lax.dot_general(a, b, (dims, ((), ())), preferred_element_type=F32)


def dot3(a, b, dims):
    return dot(a[0], b[0], dims) + (dot(a[0], b[1], dims) + dot(a[1], b[0], dims))


NT_DIMS = ((1,), (1,))
NN_DIMS = ((1,), (0,))
TN_DIMS = ((0,), (0,))


PAD = 136
CHUNKS = 4
CROWS = 2048 // CHUNKS


def spectrum_kernel(start_ref, crop_ref, x_hbm, send_ref, keep_ref, xbuf, tab_hi, tab_lo, row_hi, row_lo, sums, sem):
    grp = lax.axis_index("grp")
    start, crop, core, row0 = start_ref[0], crop_ref[0], grp & 1, grp * 128
    copies = []
    for h in range(CHUNKS):
        rows = pl.ds(CROWS * h, CROWS)
        cp = pltpu.make_async_copy(x_hbm.at[rows], xbuf.at[rows], sem.at[h])
        cp.start()
        copies.append(cp)

    flip = start & 1
    scale = 1.0 / math.sqrt(NT)

    def one_table(i, _):
        t = i * 64 + lax.broadcasted_iota(jnp.int32, (64, 128), 0)
        m = lax.broadcasted_iota(jnp.int32, (64, 128), 1)
        owner = jnp.where(m < 64, 1 - core, core)
        j = (m & 32) * 2 + owner * 32 + (m & 31)
        rows = pl.ds(pl.multiple_of(i * 64, 64), 64)
        for e in range(2):
            cos, sin = cos_sin(((start + 2 * j + (e ^ flip)) * t) & (TURN - 1))
            for part, val in ((0, cos * scale), (1, sin * -scale)):
                hi, lo = split(val)
                lanes = slice(256 * e + 128 * part, 256 * e + 128 * part + 128)
                tab_hi[rows, lanes] = hi
                tab_lo[rows, lanes] = lo
        return 0

    lax.fori_loop(0, 16, one_table, 0)

    rscale = 1.0 / math.sqrt(NR)
    r = row0 + lax.broadcasted_iota(jnp.int32, (128, CROP), 0)
    p = crop + lax.broadcasted_iota(jnp.int32, (128, CROP), 1)
    cos, sin = cos_sin(((r * p) & (NR - 1)) * (TURN // NR))
    cos, sin = cos * rscale, sin * rscale
    for rows, cols, val in ((0, 0, cos), (0, 128, -sin), (128, 0, sin), (128, 128, cos)):
        hi, lo = split(val)
        row_hi[rows : rows + 128, cols : cols + 128] = hi
        row_lo[rows : rows + 128, cols : cols + 128] = lo

    for h in range(CHUNKS):
        copies[h].wait()

        def delays(i, _):
            first = h * CROWS + i * 256
            rows = pl.ds(pl.multiple_of(first, 256), 256)
            a = xbuf[rows, 0:HALF]
            b = xbuf[rows, HALF:NT]
            for e in range(2):
                y = split(a + b if e == 0 else a - b)
                d = dot3(y, (tab_hi[:, 256 * e : 256 * e + 256], tab_lo[:, 256 * e : 256 * e + 256]), NN_DIMS)
                d = d.reshape(16, 2, 8, 256)
                at = pl.ds(pl.multiple_of(first // 2, 128), 128)
                for o in range(2):
                    for ri in range(2):
                        sums[e, o, ri, at, :] = d[:, o, :, 128 * ri : 128 * ri + 128].reshape(128, 128)
            return 0

        lax.fori_loop(0, CROWS // 256, delays, 0, unroll=2)

    def rowwise(i, _):
        for e in range(2):
            blocks = []
            for k in range(2):
                c = 2 * i + k
                s = [sums[e, c >> 3, ri, pl.ds(c & 7, 128, stride=8), :] for ri in range(2)]
                blocks.append(jnp.concatenate([s[0].T, s[1].T], axis=1))
            g = dot3(split(jnp.concatenate(blocks, axis=0)), (row_hi[...], row_lo[...]), NN_DIMS)
            for k in range(2):
                first = (e ^ flip) * 32 + 2 * i + k
                for rel, ref in ((0, send_ref), (1, keep_ref)):
                    for y in range(2):
                        at = k * 128 + rel * 64 + y * 32
                        for ri in range(2):
                            ref[pl.ds(y * 64 + ri * 16 + first, 32, stride=PAD), :] = g[
                                at : at + 32, 128 * ri : 128 * ri + 128
                            ]
        return 0

    lax.fori_loop(0, 8, rowwise, 0, unroll=4)


def spectrum_call(start, crop, x):
    out = jax.ShapeDtypeStruct((32 * PAD, 128), F32)
    smem = pl.BlockSpec(memory_space=pltpu.SMEM)
    return pl.pallas_call(
        spectrum_kernel,
        out_shape=(out, out),
        in_specs=[smem, smem, pl.BlockSpec(memory_space=pl.ANY)],
        out_specs=(pl.BlockSpec(memory_space=pltpu.VMEM), pl.BlockSpec(memory_space=pltpu.VMEM)),
        scratch_shapes=[
            pltpu.VMEM((2048, NT), F32),
            pltpu.VMEM((HALF, 512), BF16),
            pltpu.VMEM((HALF, 512), BF16),
            pltpu.VMEM((256, 256), BF16),
            pltpu.VMEM((256, 256), BF16),
            pltpu.VMEM((2, 2, 2, 1024, 128), F32),
            pltpu.SemaphoreType.DMA((CHUNKS,)),
        ],
        compiler_params=pltpu.CompilerParams(vmem_limit_bytes=48 * 2**20),
        name="spectrum",
    )(start, crop, x.reshape(2048, NT))


def focal_kernel(crop_ref, g_ref, send_ref, keep_ref, tab_hi, tab_lo):
    crop, mine = crop_ref[1], lax.axis_index("grp") >> 1
    scale = 1.0 / math.sqrt(NC)
    c = lax.broadcasted_iota(jnp.int32, (NC, CROP), 0)
    q = crop + lax.broadcasted_iota(jnp.int32, (NC, CROP), 1)
    cos, sin = cos_sin(((c * q) & (NC - 1)) * (TURN // NC))
    for lane, val in ((0, cos * scale), (128, sin * scale)):
        hi, lo = split(val)
        tab_hi[:, lane : lane + 128] = hi
        tab_lo[:, lane : lane + 128] = lo
    for rel, ref in ((0, send_ref), (1, keep_ref)):
        y = 1 - mine if rel == 0 else mine
        for e in range(2):
            g = [g_ref[:, y, e, ri, :, :].reshape(NC, CROP) for ri in range(2)]
            g = jnp.concatenate(g, axis=1)
            u = dot3(split(g), (tab_hi[...], tab_lo[...]), TN_DIMS)
            ref[0, e] = u[0:128, 0:128] + u[128:256, 128:256]
            ref[1, e] = u[128:256, 0:128] - u[0:128, 128:256]


def focal_call(crop, g):
    out = jax.ShapeDtypeStruct((2, 2, CROP, CROP), F32)
    return pl.pallas_call(
        focal_kernel,
        out_shape=(out, out),
        in_specs=[pl.BlockSpec(memory_space=pltpu.SMEM), pl.BlockSpec(memory_space=pltpu.VMEM)],
        out_specs=(pl.BlockSpec(memory_space=pltpu.VMEM), pl.BlockSpec(memory_space=pltpu.VMEM)),
        scratch_shapes=[pltpu.VMEM((NC, 256), BF16), pltpu.VMEM((NC, 256), BF16)],
        compiler_params=pltpu.CompilerParams(vmem_limit_bytes=24 * 2**20),
        name="focal",
    )(crop, g)


def on_device(interferogram, sideband_start, crop_start):
    send, keep = spectrum_call(sideband_start, crop_start, interferogram)
    got = lax.ppermute(send, "grp", [(i, i ^ 1) for i in range(4)])
    mine = (keep.reshape(32, PAD, 128) + got.reshape(32, PAD, 128))[:, :128]
    gathered = lax.all_to_all(mine, "col", split_axis=0, concat_axis=0, tiled=True)
    send, keep = focal_call(crop_start, gathered.reshape(32, 2, 2, 2, 16, 128))
    got = lax.ppermute(send, "grp", [(i, i ^ 2) for i in range(4)])
    return keep + got


def solution(mesh):
    return jax.shard_map(
        on_device,
        mesh=mesh,
        in_specs=(P("grp", "col", None), P(), P()),
        out_specs=P(None, ("grp", "col"), None, None),
        check_vma=False,
    )
```

```python
import functools
import math

import jax
import jax.numpy as jnp
from jax import lax
from jax.experimental import pallas as pl
from jax.experimental.pallas import tpu as pltpu
from jax.sharding import PartitionSpec as P

NR = 512
NC = 512
NT = 2048
NB = 256
CROP = 128
HALF = NT // 2
TURN = 2048
F32 = jnp.float32
BF16 = jnp.bfloat16


def cos_sin(u):
    v = u + 256
    quadrant = (v >> 9) & 3
    r = ((v & 511) - 256).astype(F32) * (2.0 * math.pi / TURN)
    z = r * r
    s = r + r * z * (-1.6666654611e-1 + z * (8.3321608736e-3 + z * -1.9515295891e-4))
    c = 1.0 - 0.5 * z + z * z * (4.166664568298827e-2 + z * (-1.388731625493765e-3 + z * 2.443315711809948e-5))
    odd = (quadrant & 1) == 1
    cos = jnp.where(odd, s, c)
    sin = jnp.where(odd, c, s)
    cos = jnp.where((quadrant == 1) | (quadrant == 2), -cos, cos)
    sin = jnp.where(quadrant >= 2, -sin, sin)
    return cos, sin


def split(a):
    hi = a.astype(BF16)
    return hi, (a - hi.astype(F32)).astype(BF16)


def dot(a, b, dims):
    return lax.dot_general(a, b, (dims, ((), ())), preferred_element_type=F32)


def dot3(a, b, dims):
    return dot(a[0], b[0], dims) + (dot(a[0], b[1], dims) + dot(a[1], b[0], dims))


NT_DIMS = ((1,), (1,))
NN_DIMS = ((1,), (0,))
TN_DIMS = ((0,), (0,))


PAD = 136
CHUNKS = 4
CROWS = 2048 // CHUNKS


def spectrum_kernel(
    start_ref, crop_ref, x_hbm, send_ref, keep_ref, xbuf, tab_hi, tab_lo, row_hi, row_lo, sums, sem
):
    grp = lax.axis_index("grp")
    start, crop = start_ref[0], crop_ref[0]
    core, y_lo, row0 = grp & 1, grp >> 1, grp * 128
    copies = []
    for h in range(CHUNKS):
        rows = pl.ds(CROWS * h, CROWS)
        cp = pltpu.make_async_copy(x_hbm.at[rows], xbuf.at[rows], sem.at[h])
        cp.start()
        copies.append(cp)

    flip = start & 1
    scale = 1.0 / math.sqrt(NT)

    def one_table(i, _):
        t = i * 64 + lax.broadcasted_iota(jnp.int32, (64, 128), 0)
        m = lax.broadcasted_iota(jnp.int32, (64, 128), 1)
        owner = jnp.where(m < 64, 1 - core, core)
        other = (m & 32) == 0
        half = jnp.where(other, 1 - y_lo, y_lo) * 64 + owner * 32
        rows = pl.ds(pl.multiple_of(i * 64, 64), 64)
        for e in range(2):
            odd = e ^ flip
            j = half + ((m & 31) ^ jnp.where(other, odd * 16, 0))
            cos, sin = cos_sin(((start + 2 * j + odd) * t) & (TURN - 1))
            for part, val in ((0, cos * scale), (1, sin * -scale)):
                hi, lo = split(val)
                lanes = slice(256 * e + 128 * part, 256 * e + 128 * part + 128)
                tab_hi[rows, lanes] = hi
                tab_lo[rows, lanes] = lo
        return 0

    lax.fori_loop(0, 16, one_table, 0)

    rscale = 1.0 / math.sqrt(NR)
    r = row0 + lax.broadcasted_iota(jnp.int32, (128, CROP), 0)
    p = crop + lax.broadcasted_iota(jnp.int32, (128, CROP), 1)
    cos, sin = cos_sin(((r * p) & (NR - 1)) * (TURN // NR))
    cos, sin = cos * rscale, sin * rscale
    for rows, cols, val in ((0, 0, cos), (0, 128, -sin), (128, 0, sin), (128, 128, cos)):
        hi, lo = split(val)
        row_hi[rows : rows + 128, cols : cols + 128] = hi
        row_lo[rows : rows + 128, cols : cols + 128] = lo

    for h in range(CHUNKS):
        copies[h].wait()

        def delays(i, _):
            first = h * CROWS + i * 256
            rows = pl.ds(pl.multiple_of(first, 256), 256)
            a = xbuf[rows, 0:HALF]
            b = xbuf[rows, HALF:NT]
            for e in range(2):
                y = split(a + b if e == 0 else a - b)
                d = dot3(y, (tab_hi[:, 256 * e : 256 * e + 256], tab_lo[:, 256 * e : 256 * e + 256]), NN_DIMS)
                d = d.reshape(16, 2, 8, 256)
                at = pl.ds(pl.multiple_of(first // 2, 128), 128)
                for o in range(2):
                    for ri in range(2):
                        sums[e, o, ri, at, :] = d[:, o, :, 128 * ri : 128 * ri + 128].reshape(128, 128)
            return 0

        lax.fori_loop(0, CROWS // 256, delays, 0, unroll=2)

    def rowwise(i, _):
        for e in range(2):
            blocks = []
            for k in range(2):
                c = 2 * i + k
                s = [sums[e, c >> 3, ri, pl.ds(c & 7, 128, stride=8), :] for ri in range(2)]
                blocks.append(jnp.concatenate([s[0].T, s[1].T], axis=1))
            g = dot3(split(jnp.concatenate(blocks, axis=0)), (row_hi[...], row_lo[...]), NN_DIMS)
            for k in range(2):
                first = (e ^ flip) * 32 + 2 * i + k
                for rel, ref in ((0, send_ref), (1, keep_ref)):
                    for y in range(2):
                        at = k * 128 + rel * 64 + y * 32
                        for ri in range(2):
                            ref[pl.ds(y * 64 + ri * 16 + first, 32, stride=PAD), :] = g[
                                at : at + 32, 128 * ri : 128 * ri + 128
                            ]
        return 0

    lax.fori_loop(0, 8, rowwise, 0, unroll=4)


def spectrum_call(start, crop, x):
    out = jax.ShapeDtypeStruct((32 * PAD, 128), F32)
    smem = pl.BlockSpec(memory_space=pltpu.SMEM)
    return pl.pallas_call(
        spectrum_kernel,
        out_shape=(out, out),
        in_specs=[smem, smem, pl.BlockSpec(memory_space=pl.ANY)],
        out_specs=(pl.BlockSpec(memory_space=pltpu.VMEM), pl.BlockSpec(memory_space=pltpu.VMEM)),
        scratch_shapes=[
            pltpu.VMEM((2048, NT), F32),
            pltpu.VMEM((HALF, 512), BF16),
            pltpu.VMEM((HALF, 512), BF16),
            pltpu.VMEM((256, 256), BF16),
            pltpu.VMEM((256, 256), BF16),
            pltpu.VMEM((2, 2, 2, 1024, 128), F32),
            pltpu.SemaphoreType.DMA((CHUNKS,)),
        ],
        compiler_params=pltpu.CompilerParams(vmem_limit_bytes=48 * 2**20),
        name="spectrum",
    )(start, crop, x.reshape(2048, NT))


def table_kernel(crop_ref, hi_ref, lo_ref):
    scale = 1.0 / math.sqrt(NC)
    c = lax.broadcasted_iota(jnp.int32, (NC, CROP), 0)
    q = crop_ref[1] + lax.broadcasted_iota(jnp.int32, (NC, CROP), 1)
    cos, sin = cos_sin(((c * q) & (NC - 1)) * (TURN // NC))
    for lane, val in ((0, cos * scale), (128, sin * scale)):
        hi, lo = split(val)
        hi_ref[:, lane : lane + 128] = hi
        lo_ref[:, lane : lane + 128] = lo


def table_call(crop):
    out = jax.ShapeDtypeStruct((NC, 256), BF16)
    return pl.pallas_call(
        table_kernel,
        out_shape=(out, out),
        in_specs=[pl.BlockSpec(memory_space=pltpu.SMEM)],
        out_specs=(pl.BlockSpec(memory_space=pltpu.VMEM),) * 2,
        cost_estimate=pl.CostEstimate(flops=4_000_000, bytes_accessed=4_000_000, transcendentals=0),
        compiler_params=pltpu.CompilerParams(vmem_limit_bytes=8 * 2**20),
        name="table",
    )(crop)


def focal_kernel(whose, hi_ref, lo_ref, g_ref, *outs):
    for e in range(2):
        g = [g_ref[:, whose, e, ri, :, :].reshape(NC, CROP) for ri in range(2)]
        u = dot3(split(jnp.concatenate(g, axis=1)), (hi_ref[...], lo_ref[...]), TN_DIMS)
        real = u[0:128, 0:128] + u[128:256, 128:256]
        imag = u[128:256, 0:128] - u[0:128, 128:256]
        if len(outs) == 2:
            outs[e][0], outs[e][1] = real, imag
        else:
            outs[0][0, e], outs[0][1, e] = real, imag


def focal_call(whose, table, g):
    if whose == 0:
        out = (jax.ShapeDtypeStruct((2, CROP, CROP), F32),) * 2
    else:
        out = (jax.ShapeDtypeStruct((2, 2, CROP, CROP), F32),)
    return pl.pallas_call(
        functools.partial(focal_kernel, whose),
        out_shape=out,
        in_specs=[pl.BlockSpec(memory_space=pltpu.VMEM)] * 3,
        out_specs=(pl.BlockSpec(memory_space=pltpu.VMEM),) * len(out),
        cost_estimate=pl.CostEstimate(flops=400_000_000, bytes_accessed=4_000_000, transcendentals=0),
        compiler_params=pltpu.CompilerParams(vmem_limit_bytes=24 * 2**20),
        name="focal_send" if whose == 0 else "focal_keep",
    )(*table, g)


def sum_kernel(keep_ref, even_ref, odd_ref, out_ref):
    for e, ref in ((0, even_ref), (1, odd_ref)):
        for ri in range(2):
            out_ref[ri, e] = keep_ref[ri, e] + ref[ri]


def sum_call(keep, even, odd):
    return pl.pallas_call(
        sum_kernel,
        out_shape=jax.ShapeDtypeStruct((2, 2, CROP, CROP), F32),
        in_specs=[pl.BlockSpec(memory_space=pltpu.VMEM)] * 3,
        out_specs=pl.BlockSpec(memory_space=pltpu.VMEM),
        compiler_params=pltpu.CompilerParams(vmem_limit_bytes=4 * 2**20),
        name="sum",
    )(keep, even, odd)


def on_device(interferogram, sideband_start, crop_start):
    send, keep = spectrum_call(sideband_start, crop_start, interferogram)
    got = lax.ppermute(send, "grp", [(i, i ^ 1) for i in range(4)])
    got, table = lax.optimization_barrier((got, table_call(crop_start)))
    mine = (keep.reshape(32, PAD, 128) + got.reshape(32, PAD, 128))[:, :128]
    gathered = lax.all_to_all(mine, "col", split_axis=0, concat_axis=0, tiled=True)
    gathered = gathered.reshape(32, 2, 2, 2, 16, 128)
    even, odd = focal_call(0, table, gathered)
    near = [(i, i ^ 64) for i in range(128)]
    far = [(i, i ^ 64 ^ 16) for i in range(128)]
    even = lax.ppermute(even, ("grp", "col"), near)
    odd = lax.ppermute(odd, ("grp", "col"), far)
    (keep,) = focal_call(1, table, gathered)
    return sum_call(keep, even, odd)


def solution(mesh):
    return jax.shard_map(
        on_device,
        mesh=mesh,
        in_specs=(P("grp", "col", None), P(), P()),
        out_specs=P(None, ("grp", "col"), None, None),
        check_vma=False,
    )
```

```python
import functools
import math

import jax
import jax.numpy as jnp
from jax import lax
from jax.experimental import pallas as pl
from jax.experimental.pallas import tpu as pltpu
from jax.sharding import PartitionSpec as P

NR = 512
NC = 512
NT = 2048
NB = 256
CROP = 128
TURN = 2048
F32 = jnp.float32
BF16 = jnp.bfloat16


def cos_sin(u):
    v = u + 256
    quadrant = (v >> 9) & 3
    r = ((v & 511) - 256).astype(F32) * (2.0 * math.pi / TURN)
    z = r * r
    s = r + r * z * (-1.6666654611e-1 + z * (8.3321608736e-3 + z * -1.9515295891e-4))
    c = 1.0 - 0.5 * z + z * z * (4.166664568298827e-2 + z * (-1.388731625493765e-3 + z * 2.443315711809948e-5))
    odd = (quadrant & 1) == 1
    cos = jnp.where(odd, s, c)
    sin = jnp.where(odd, c, s)
    cos = jnp.where((quadrant == 1) | (quadrant == 2), -cos, cos)
    sin = jnp.where(quadrant >= 2, -sin, sin)
    return cos, sin


def split(a):
    hi = a.astype(BF16)
    return hi, (a - hi.astype(F32)).astype(BF16)


def dot(a, b, dims):
    return lax.dot_general(a, b, (dims, ((), ())), preferred_element_type=F32)


def dot3(a, b, dims):
    return dot(a[0], b[0], dims) + (dot(a[0], b[1], dims) + dot(a[1], b[0], dims))


NT_DIMS = ((1,), (1,))
NN_DIMS = ((1,), (0,))
TN_DIMS = ((0,), (0,))


PAD = 136
CHUNKS = 2
CROWS = 128 // CHUNKS
FOLD = NT // 8
GROUPS = (((0, 4), 0), ((2, 6), -1), ((1, 7), -1), ((3, 5), 1))


def folded(x):
    s = [x[j] + x[j + 4] for j in range(4)]
    d = [x[j] - x[j + 4] for j in range(4)]
    p, q = s[0] + s[2], s[1] + s[3]
    u, v = (d[1] - d[3]) * math.sqrt(0.5), (d[1] + d[3]) * math.sqrt(0.5)
    return ((p + q, p - q), (s[0] - s[2], s[1] - s[3]), (d[0] + u, d[2] + v), (d[0] - u, d[2] - v))


def spectrum_kernel(start_ref, crop_ref, x_hbm, send_ref, keep_ref, xbuf, table, row_hi, row_lo, sums, sem):
    grp = lax.axis_index("grp")
    start, crop = start_ref[0], crop_ref[0]
    core, y_lo, row0 = grp & 1, grp >> 1, grp * 128
    copies = []
    for o in range(2):
        for h in range(CHUNKS):
            rows = pl.ds(CROWS * h, CROWS)
            cp = pltpu.make_async_copy(x_hbm.at[rows, o], xbuf.at[o, rows], sem.at[o, h])
            cp.start()
            copies.append(cp)

    scale = 1.0 / math.sqrt(NT)

    lane = lax.broadcasted_iota(jnp.int32, (1, 128), 1)
    real, first = lane < 64, (lane & 32) == 0
    owner = jnp.where((lane & 16) == 0, 1 - core, core)
    other = (lane & 8) == 0
    half = jnp.where(other, 1 - y_lo, y_lo)
    for g, (residues, sign) in enumerate(GROUPS):
        kappa = (jnp.where(first, residues[0], residues[1]) - start) & 7
        flip = jnp.where(other, (kappa & 1) * 4, 0)
        freq = start + kappa + 8 * (half * 16 + owner * 8 + ((lane & 7) ^ flip))

        def one_table(i, _, g=g, sign=sign, freq=freq):
            t = i * 64 + lax.broadcasted_iota(jnp.int32, (64, 128), 0)
            cos, sin = cos_sin((freq * t) & (TURN - 1))
            cos, sin = cos * scale, sin * scale
            a = jnp.where(real, cos, -sin)
            if sign == 0:
                a, b = jnp.where(first, a, 0.0), jnp.where(first, 0.0, a)
            else:
                b = jnp.where(real, sin, cos) * jnp.where(first, float(sign), float(-sign))
            for at, val in ((0, a), (FOLD, b)):
                hi, lo = split(val)
                rows = pl.ds(pl.multiple_of(at + i * 64, 64), 64)
                table[g, rows, 0:128] = hi
                table[g, rows, 128:256] = lo
            return 0

        lax.fori_loop(0, FOLD // 64, one_table, 0)

    rscale = 1.0 / math.sqrt(NR)
    r = row0 + lax.broadcasted_iota(jnp.int32, (128, CROP), 0)
    p = crop + lax.broadcasted_iota(jnp.int32, (128, CROP), 1)
    cos, sin = cos_sin(((r * p) & (NR - 1)) * (TURN // NR))
    cos, sin = cos * rscale, sin * rscale
    for rows, cols, val in ((0, 0, cos), (0, 128, -sin), (128, 0, sin), (128, 128, cos)):
        hi, lo = split(val)
        row_hi[rows : rows + 128, cols : cols + 128] = hi
        row_lo[rows : rows + 128, cols : cols + 128] = lo

    base = []
    for residues, _ in GROUPS:
        for residue in residues:
            kappa = (residue - start) & 7
            base.append((kappa >> 1) * (8 * PAD) + (kappa & 1) * 32)

    for o in range(2):
        for h in range(CHUNKS):
            copies[o * CHUNKS + h].wait()
            pixels = xbuf.at[o].reshape(1024, NT)

            def delays(i, _, h=h, pixels=pixels):
                rows = pl.ds(pl.multiple_of(h * CROWS * 8 + i * 256, 256), 256)
                inputs = folded([pixels[rows, FOLD * j : FOLD * (j + 1)] for j in range(8)])
                for g in range(4):
                    hi, lo = split(jnp.concatenate(inputs[g], axis=1))
                    d = dot(hi, table[g], NN_DIMS) + dot(lo, table[g], NN_DIMS)
                    sums[g, rows, :] = d[:, 0:128] + d[:, 128:256]
                return 0

            lax.fori_loop(0, CROWS // 32, delays, 0, unroll=2)

        def rowwise(c, _, o=o):
            blocks = []
            for g in range(4):
                s = sums[g, pl.ds(c, 128, stride=8), :].T
                blocks.append(jnp.concatenate([s[0:64], s[64:128]], axis=1))
            f = dot3(split(jnp.concatenate(blocks, axis=0)), (row_hi[...], row_lo[...]), NN_DIMS)
            for n in range(8):
                for rel, ref in ((0, send_ref), (1, keep_ref)):
                    for y in range(2):
                        at = n * 32 + rel * 16 + y * 8
                        for ri in range(2):
                            ref[pl.ds(base[n] + (y * 64 + ri * 16 + o * 8 + c), 8, stride=PAD), :] = f[
                                at : at + 8, 128 * ri : 128 * ri + 128
                            ]
            return 0

        lax.fori_loop(0, 8, rowwise, 0, unroll=True)


def spectrum_call(start, crop, x):
    out = jax.ShapeDtypeStruct((32 * PAD, 128), F32)
    smem = pl.BlockSpec(memory_space=pltpu.SMEM)
    return pl.pallas_call(
        spectrum_kernel,
        out_shape=(out, out),
        in_specs=[smem, smem, pl.BlockSpec(memory_space=pl.ANY)],
        out_specs=(pl.BlockSpec(memory_space=pltpu.VMEM), pl.BlockSpec(memory_space=pltpu.VMEM)),
        scratch_shapes=[
            pltpu.VMEM((2, 128, 8, NT), F32),
            pltpu.VMEM((4, 2 * FOLD, 256), BF16),
            pltpu.VMEM((256, 256), BF16),
            pltpu.VMEM((256, 256), BF16),
            pltpu.VMEM((4, 1024, 128), F32),
            pltpu.SemaphoreType.DMA((2, CHUNKS)),
        ],
        compiler_params=pltpu.CompilerParams(vmem_limit_bytes=48 * 2**20),
        name="spectrum",
    )(start, crop, x.reshape(128, 2, 8, NT))


def table_kernel(crop_ref, hi_ref, lo_ref):
    scale = 1.0 / math.sqrt(NC)
    c = lax.broadcasted_iota(jnp.int32, (NC, CROP), 0)
    q = crop_ref[1] + lax.broadcasted_iota(jnp.int32, (NC, CROP), 1)
    cos, sin = cos_sin(((c * q) & (NC - 1)) * (TURN // NC))
    for lane, val in ((0, cos * scale), (128, sin * scale)):
        hi, lo = split(val)
        hi_ref[:, lane : lane + 128] = hi
        lo_ref[:, lane : lane + 128] = lo


def table_call(crop):
    out = jax.ShapeDtypeStruct((NC, 256), BF16)
    return pl.pallas_call(
        table_kernel,
        out_shape=(out, out),
        in_specs=[pl.BlockSpec(memory_space=pltpu.SMEM)],
        out_specs=(pl.BlockSpec(memory_space=pltpu.VMEM),) * 2,
        cost_estimate=pl.CostEstimate(flops=4_000_000, bytes_accessed=4_000_000, transcendentals=0),
        compiler_params=pltpu.CompilerParams(vmem_limit_bytes=8 * 2**20),
        name="table",
    )(crop)


def focal_kernel(whose, hi_ref, lo_ref, g_ref, *outs):
    for e in range(2):
        g = [g_ref[:, whose, e, ri, :, :].reshape(NC, CROP) for ri in range(2)]
        u = dot3(split(jnp.concatenate(g, axis=1)), (hi_ref[...], lo_ref[...]), TN_DIMS)
        real = u[0:128, 0:128] + u[128:256, 128:256]
        imag = u[128:256, 0:128] - u[0:128, 128:256]
        if len(outs) == 2:
            outs[e][0], outs[e][1] = real, imag
        else:
            outs[0][0, e], outs[0][1, e] = real, imag


def focal_call(whose, table, g):
    if whose == 0:
        out = (jax.ShapeDtypeStruct((2, CROP, CROP), F32),) * 2
    else:
        out = (jax.ShapeDtypeStruct((2, 2, CROP, CROP), F32),)
    return pl.pallas_call(
        functools.partial(focal_kernel, whose),
        out_shape=out,
        in_specs=[pl.BlockSpec(memory_space=pltpu.VMEM)] * 3,
        out_specs=(pl.BlockSpec(memory_space=pltpu.VMEM),) * len(out),
        cost_estimate=pl.CostEstimate(flops=400_000_000, bytes_accessed=4_000_000, transcendentals=0),
        compiler_params=pltpu.CompilerParams(vmem_limit_bytes=24 * 2**20),
        name="focal_send" if whose == 0 else "focal_keep",
    )(*table, g)


def sum_kernel(keep_ref, even_ref, odd_ref, out_ref):
    for e, ref in ((0, even_ref), (1, odd_ref)):
        for ri in range(2):
            out_ref[ri, e] = keep_ref[ri, e] + ref[ri]


def sum_call(keep, even, odd):
    return pl.pallas_call(
        sum_kernel,
        out_shape=jax.ShapeDtypeStruct((2, 2, CROP, CROP), F32),
        in_specs=[pl.BlockSpec(memory_space=pltpu.VMEM)] * 3,
        out_specs=pl.BlockSpec(memory_space=pltpu.VMEM),
        compiler_params=pltpu.CompilerParams(vmem_limit_bytes=4 * 2**20),
        name="sum",
    )(keep, even, odd)


def on_device(interferogram, sideband_start, crop_start):
    send, keep = spectrum_call(sideband_start, crop_start, interferogram)
    got = lax.ppermute(send, "grp", [(i, i ^ 1) for i in range(4)])
    got, table = lax.optimization_barrier((got, table_call(crop_start)))
    mine = (keep + got).reshape(4, 8, PAD, 128)[:, :, :128]
    mine = mine.transpose(1, 0, 2, 3).reshape(32, 128, 128)
    gathered = lax.all_to_all(mine, "col", split_axis=0, concat_axis=0, tiled=True)
    gathered = gathered.reshape(32, 2, 2, 2, 16, 128)
    even, odd = focal_call(0, table, gathered)
    near = [(i, i ^ 64) for i in range(128)]
    far = [(i, i ^ 64 ^ 16) for i in range(128)]
    even = lax.ppermute(even, ("grp", "col"), near)
    odd = lax.ppermute(odd, ("grp", "col"), far)
    (keep,) = focal_call(1, table, gathered)
    return sum_call(keep, even, odd)


def solution(mesh):
    return jax.shard_map(
        on_device,
        mesh=mesh,
        in_specs=(P("grp", "col", None), P(), P()),
        out_specs=P(None, ("grp", "col"), None, None),
        check_vma=False,
    )
```

```python
import functools
import math

import jax
import jax.numpy as jnp
from jax import lax
from jax.experimental import pallas as pl
from jax.experimental.pallas import tpu as pltpu
from jax.sharding import PartitionSpec as P

NR = 512
NC = 512
NT = 2048
NB = 256
CROP = 128
TURN = 2048
F32 = jnp.float32
BF16 = jnp.bfloat16


def cos_sin(u):
    v = u + 256
    quadrant = (v >> 9) & 3
    r = ((v & 511) - 256).astype(F32) * (2.0 * math.pi / TURN)
    z = r * r
    s = r + r * z * (-1.6666654611e-1 + z * (8.3321608736e-3 + z * -1.9515295891e-4))
    c = 1.0 - 0.5 * z + z * z * (4.166664568298827e-2 + z * (-1.388731625493765e-3 + z * 2.443315711809948e-5))
    odd = (quadrant & 1) == 1
    cos = jnp.where(odd, s, c)
    sin = jnp.where(odd, c, s)
    cos = jnp.where((quadrant == 1) | (quadrant == 2), -cos, cos)
    sin = jnp.where(quadrant >= 2, -sin, sin)
    return cos, sin


def split(a):
    hi = a.astype(BF16)
    return hi, (a - hi.astype(F32)).astype(BF16)


def dot(a, b, dims):
    return lax.dot_general(a, b, (dims, ((), ())), preferred_element_type=F32)


def dot3(a, b, dims):
    return dot(a[0], b[0], dims) + (dot(a[0], b[1], dims) + dot(a[1], b[0], dims))


NT_DIMS = ((1,), (1,))
NN_DIMS = ((1,), (0,))
TN_DIMS = ((0,), (0,))


CHUNKS = 2
CROWS = 128 // CHUNKS
FOLD = NT // 8
GROUPS = (((0, 4), 0), ((2, 6), -1), ((1, 7), -1), ((3, 5), 1))


def folded(x):
    s = [x[j] + x[j + 4] for j in range(4)]
    d = [x[j] - x[j + 4] for j in range(4)]
    p, q = s[0] + s[2], s[1] + s[3]
    u, v = (d[1] - d[3]) * math.sqrt(0.5), (d[1] + d[3]) * math.sqrt(0.5)
    return ((p + q, p - q), (s[0] - s[2], s[1] - s[3]), (d[0] + u, d[2] + v), (d[0] - u, d[2] - v))


def row_stage(start, sums, row_hi, row_lo, send_ref, keep_ref):
    base = []
    for residues, _ in GROUPS:
        for residue in residues:
            kappa = (residue - start) & 7
            base.append((kappa >> 1) * 64 + (kappa & 1) * 512)

    def rowwise(c, _):
        blocks = []
        for g in range(4):
            s = sums[g, pl.ds(c, 128, stride=8), :].T
            blocks.append(jnp.concatenate([s[0:64], s[64:128]], axis=1))
        f = dot3(split(jnp.concatenate(blocks, axis=0)), (row_hi[...], row_lo[...]), NN_DIMS)
        for n in range(8):
            for rel, ref in ((0, send_ref), (1, keep_ref)):
                for y in range(2):
                    at = n * 32 + rel * 16 + y * 8
                    for ri in range(2):
                        ref[pl.ds(base[n] + (y * 1024 + ri * 256 + c), 8, stride=8), :] = f[
                            at : at + 8, 128 * ri : 128 * ri + 128
                        ]
        return 0

    lax.fori_loop(0, 8, rowwise, 0, unroll=True)


def spectrum_kernel(
    start_ref, crop_ref, x_hbm, send_ref, keep_ref, later_ref, row_hi, row_lo, xbuf, table, sums, sem
):
    grp = lax.axis_index("grp")
    start, crop = start_ref[0], crop_ref[0]
    core, y_lo, row0 = grp & 1, grp >> 1, grp * 128
    copies = []
    for o in range(2):
        for h in range(CHUNKS):
            rows = pl.ds(CROWS * h, CROWS)
            cp = pltpu.make_async_copy(x_hbm.at[rows, o], xbuf.at[o, rows], sem.at[o, h])
            cp.start()
            copies.append(cp)

    scale = 1.0 / math.sqrt(NT)

    lane = lax.broadcasted_iota(jnp.int32, (1, 128), 1)
    real, first = lane < 64, (lane & 32) == 0
    owner = jnp.where((lane & 16) == 0, 1 - core, core)
    other = (lane & 8) == 0
    half = jnp.where(other, 1 - y_lo, y_lo)
    for g, (residues, sign) in enumerate(GROUPS):
        kappa = (jnp.where(first, residues[0], residues[1]) - start) & 7
        flip = jnp.where(other, (kappa & 1) * 4, 0)
        freq = start + kappa + 8 * (half * 16 + owner * 8 + ((lane & 7) ^ flip))

        def one_table(i, _, g=g, sign=sign, freq=freq):
            t = i * 64 + lax.broadcasted_iota(jnp.int32, (64, 128), 0)
            cos, sin = cos_sin((freq * t) & (TURN - 1))
            cos, sin = cos * scale, sin * scale
            a = jnp.where(real, cos, -sin)
            if sign == 0:
                a, b = jnp.where(first, a, 0.0), jnp.where(first, 0.0, a)
            else:
                b = jnp.where(real, sin, cos) * jnp.where(first, float(sign), float(-sign))
            for at, val in ((0, a), (FOLD, b)):
                hi, lo = split(val)
                rows = pl.ds(pl.multiple_of(at + i * 64, 64), 64)
                table[g, rows, 0:128] = hi
                table[g, rows, 128:256] = lo
            return 0

        lax.fori_loop(0, FOLD // 64, one_table, 0)

    rscale = 1.0 / math.sqrt(NR)
    r = row0 + lax.broadcasted_iota(jnp.int32, (128, CROP), 0)
    p = crop + lax.broadcasted_iota(jnp.int32, (128, CROP), 1)
    cos, sin = cos_sin(((r * p) & (NR - 1)) * (TURN // NR))
    cos, sin = cos * rscale, sin * rscale
    for rows, cols, val in ((0, 0, cos), (0, 128, -sin), (128, 0, sin), (128, 128, cos)):
        hi, lo = split(val)
        row_hi[rows : rows + 128, cols : cols + 128] = hi
        row_lo[rows : rows + 128, cols : cols + 128] = lo

    for o, spectra in ((0, sums), (1, later_ref)):
        for h in range(CHUNKS):
            copies[o * CHUNKS + h].wait()
            pixels = xbuf.at[o].reshape(1024, NT)

            def delays(i, _, h=h, pixels=pixels, spectra=spectra):
                rows = pl.ds(pl.multiple_of(h * CROWS * 8 + i * 256, 256), 256)
                inputs = folded([pixels[rows, FOLD * j : FOLD * (j + 1)] for j in range(8)])
                for g in range(4):
                    hi, lo = split(jnp.concatenate(inputs[g], axis=1))
                    d = dot(hi, table[g], NN_DIMS) + dot(lo, table[g], NN_DIMS)
                    spectra[g, rows, :] = d[:, 0:128] + d[:, 128:256]
                return 0

            lax.fori_loop(0, CROWS // 32, delays, 0, unroll=2)
        if o == 0:
            row_stage(start, sums, row_hi, row_lo, send_ref, keep_ref)


VMEM = pl.BlockSpec(memory_space=pltpu.VMEM)
SMEM = pl.BlockSpec(memory_space=pltpu.SMEM)
OCTET = jax.ShapeDtypeStruct((2048, 128), F32)


def spectrum_call(start, crop, x):
    return pl.pallas_call(
        spectrum_kernel,
        out_shape=(
            OCTET,
            OCTET,
            jax.ShapeDtypeStruct((4, 1024, 128), F32),
            jax.ShapeDtypeStruct((256, 256), BF16),
            jax.ShapeDtypeStruct((256, 256), BF16),
        ),
        in_specs=[SMEM, SMEM, pl.BlockSpec(memory_space=pl.ANY)],
        out_specs=(VMEM,) * 5,
        scratch_shapes=[
            pltpu.VMEM((2, 128, 8, NT), F32),
            pltpu.VMEM((4, 2 * FOLD, 256), BF16),
            pltpu.VMEM((4, 1024, 128), F32),
            pltpu.SemaphoreType.DMA((2, CHUNKS)),
        ],
        compiler_params=pltpu.CompilerParams(vmem_limit_bytes=40 * 2**20),
        name="spectrum",
    )(start, crop, x.reshape(128, 2, 8, NT))


def row_kernel(start_ref, sums, row_hi, row_lo, send_ref, keep_ref):
    row_stage(start_ref[0], sums, row_hi, row_lo, send_ref, keep_ref)


def row_call(start, sums, row_hi, row_lo):
    return pl.pallas_call(
        row_kernel,
        out_shape=(OCTET, OCTET),
        in_specs=[SMEM, VMEM, VMEM, VMEM],
        out_specs=(VMEM, VMEM),
        cost_estimate=pl.CostEstimate(flops=800_000_000, bytes_accessed=4_000_000, transcendentals=0),
        compiler_params=pltpu.CompilerParams(vmem_limit_bytes=16 * 2**20),
        name="rows",
    )(start, sums, row_hi, row_lo)


def assemble_kernel(keep0, got0, keep1, got1, out_ref):
    for o, (a, b) in enumerate(((keep0, got0), (keep1, got1))):
        for sub in range(8):
            out_ref[:, :, sub, o] = (a[sub] + b[sub]).transpose(1, 0, 2, 3)


def assemble_call(*parts):
    return pl.pallas_call(
        assemble_kernel,
        out_shape=jax.ShapeDtypeStruct((8, 4, 8, 2, 8, 128), F32),
        in_specs=[VMEM] * 4,
        out_specs=VMEM,
        compiler_params=pltpu.CompilerParams(vmem_limit_bytes=8 * 2**20),
        name="assemble",
    )(*(p.reshape(8, 4, 8, 8, 128) for p in parts))


def table_kernel(crop_ref, after_ref, hi_ref, lo_ref):
    del after_ref
    scale = 1.0 / math.sqrt(NC)
    c = lax.broadcasted_iota(jnp.int32, (NC, CROP), 0)
    q = crop_ref[1] + lax.broadcasted_iota(jnp.int32, (NC, CROP), 1)
    cos, sin = cos_sin(((c * q) & (NC - 1)) * (TURN // NC))
    for lane, val in ((0, cos * scale), (128, sin * scale)):
        hi, lo = split(val)
        hi_ref[:, lane : lane + 128] = hi
        lo_ref[:, lane : lane + 128] = lo


def table_call(crop, after):
    out = jax.ShapeDtypeStruct((NC, 256), BF16)
    return pl.pallas_call(
        table_kernel,
        out_shape=(out, out),
        in_specs=[SMEM, pl.BlockSpec(memory_space=pl.ANY)],
        out_specs=(pl.BlockSpec(memory_space=pltpu.VMEM),) * 2,
        cost_estimate=pl.CostEstimate(flops=4_000_000, bytes_accessed=4_000_000, transcendentals=0),
        compiler_params=pltpu.CompilerParams(vmem_limit_bytes=8 * 2**20),
        name="table",
    )(crop, after)


def focal_kernel(whose, hi_ref, lo_ref, g_ref, *outs):
    for e in range(2):
        g = [g_ref[:, whose, e, ri, :, :].reshape(NC, CROP) for ri in range(2)]
        u = dot3(split(jnp.concatenate(g, axis=1)), (hi_ref[...], lo_ref[...]), TN_DIMS)
        real = u[0:128, 0:128] + u[128:256, 128:256]
        imag = u[128:256, 0:128] - u[0:128, 128:256]
        if len(outs) == 2:
            outs[e][0], outs[e][1] = real, imag
        else:
            outs[0][0, e], outs[0][1, e] = real, imag


def focal_call(whose, table, g):
    if whose == 0:
        out = (jax.ShapeDtypeStruct((2, CROP, CROP), F32),) * 2
    else:
        out = (jax.ShapeDtypeStruct((2, 2, CROP, CROP), F32),)
    return pl.pallas_call(
        functools.partial(focal_kernel, whose),
        out_shape=out,
        in_specs=[pl.BlockSpec(memory_space=pltpu.VMEM)] * 3,
        out_specs=(pl.BlockSpec(memory_space=pltpu.VMEM),) * len(out),
        cost_estimate=pl.CostEstimate(flops=400_000_000, bytes_accessed=4_000_000, transcendentals=0),
        compiler_params=pltpu.CompilerParams(vmem_limit_bytes=24 * 2**20),
        name="focal_send" if whose == 0 else "focal_keep",
    )(*table, g)


def sum_kernel(keep_ref, even_ref, odd_ref, out_ref):
    for e, ref in ((0, even_ref), (1, odd_ref)):
        for ri in range(2):
            out_ref[ri, e] = keep_ref[ri, e] + ref[ri]


def sum_call(keep, even, odd):
    return pl.pallas_call(
        sum_kernel,
        out_shape=jax.ShapeDtypeStruct((2, 2, CROP, CROP), F32),
        in_specs=[pl.BlockSpec(memory_space=pltpu.VMEM)] * 3,
        out_specs=pl.BlockSpec(memory_space=pltpu.VMEM),
        compiler_params=pltpu.CompilerParams(vmem_limit_bytes=4 * 2**20),
        name="sum",
    )(keep, even, odd)


def on_device(interferogram, sideband_start, crop_start):
    swap = [(i, i ^ 1) for i in range(4)]
    send0, keep0, later, *row_table = spectrum_call(sideband_start, crop_start, interferogram)
    got0 = lax.ppermute(send0, "grp", swap)
    send1, keep1 = row_call(sideband_start, later, *row_table)
    got1 = lax.ppermute(send1, "grp", swap)
    got1, table = lax.optimization_barrier((got1, table_call(crop_start, got0)))
    mine = assemble_call(keep0, got0, keep1, got1).reshape(32, 128, 128)
    gathered = lax.all_to_all(mine, "col", split_axis=0, concat_axis=0, tiled=True)
    gathered = gathered.reshape(32, 2, 2, 2, 16, 128)
    even, odd = focal_call(0, table, gathered)
    near = [(i, i ^ 64) for i in range(128)]
    far = [(i, i ^ 64 ^ 16) for i in range(128)]
    even = lax.ppermute(even, ("grp", "col"), near)
    odd = lax.ppermute(odd, ("grp", "col"), far)
    (keep,) = focal_call(1, table, gathered)
    return sum_call(keep, even, odd)


def solution(mesh):
    return jax.shard_map(
        on_device,
        mesh=mesh,
        in_specs=(P("grp", "col", None), P(), P()),
        out_specs=P(None, ("grp", "col"), None, None),
        check_vma=False,
    )
```

```python
import functools
import math

import jax
import jax.numpy as jnp
from jax import lax
from jax.experimental import pallas as pl
from jax.experimental.pallas import tpu as pltpu
from jax.sharding import Mesh
from jax.sharding import PartitionSpec as P

NR = 512
NC = 512
NT = 2048
NB = 256
CROP = 128
TURN = 2048
F32 = jnp.float32
BF16 = jnp.bfloat16


def cos_sin(u):
    v = u + 256
    quadrant = (v >> 9) & 3
    r = ((v & 511) - 256).astype(F32) * (2.0 * math.pi / TURN)
    z = r * r
    s = r + r * z * (-1.6666654611e-1 + z * (8.3321608736e-3 + z * -1.9515295891e-4))
    c = 1.0 - 0.5 * z + z * z * (4.166664568298827e-2 + z * (-1.388731625493765e-3 + z * 2.443315711809948e-5))
    odd = (quadrant & 1) == 1
    cos = jnp.where(odd, s, c)
    sin = jnp.where(odd, c, s)
    cos = jnp.where((quadrant == 1) | (quadrant == 2), -cos, cos)
    sin = jnp.where(quadrant >= 2, -sin, sin)
    return cos, sin


def split(a):
    hi = a.astype(BF16)
    return hi, (a - hi.astype(F32)).astype(BF16)


def dot(a, b, dims):
    return lax.dot_general(a, b, (dims, ((), ())), preferred_element_type=F32)


def dot3(a, b, dims):
    return dot(a[0], b[0], dims) + (dot(a[0], b[1], dims) + dot(a[1], b[0], dims))


NT_DIMS = ((1,), (1,))
NN_DIMS = ((1,), (0,))
TN_DIMS = ((0,), (0,))


CHUNKS = (((0, 32), (32, 32), (64, 64)), ((0, 64), (64, 64)))
FOLD = NT // 8
GROUPS = (((0, 4), 0), ((2, 6), -1), ((1, 7), -1), ((3, 5), 1))


def folded(x):
    s = [x[j] + x[j + 4] for j in range(4)]
    d = [x[j] - x[j + 4] for j in range(4)]
    p, q = s[0] + s[2], s[1] + s[3]
    u, v = (d[1] - d[3]) * math.sqrt(0.5), (d[1] + d[3]) * math.sqrt(0.5)
    return ((p + q, p - q), (s[0] - s[2], s[1] - s[3]), (d[0] + u, d[2] + v), (d[0] - u, d[2] - v))


def row_stage(start, sums, row_hi, row_lo, send_ref, keep_ref):
    base = []
    for residues, _ in GROUPS:
        for residue in residues:
            kappa = (residue - start) & 7
            base.append((kappa >> 1) * 64 + (kappa & 1) * 512)

    def rowwise(c, _):
        blocks = []
        for g in range(4):
            s = sums[g, pl.ds(c, 128, stride=8), :].T
            blocks.append(jnp.concatenate([s[0:64], s[64:128]], axis=1))
        f = dot3(split(jnp.concatenate(blocks, axis=0)), (row_hi[...], row_lo[...]), NN_DIMS)
        for n in range(8):
            for rel, ref in ((0, send_ref), (1, keep_ref)):
                for y in range(2):
                    at = n * 32 + rel * 16 + y * 8
                    for ri in range(2):
                        ref[pl.ds(base[n] + (y * 1024 + ri * 256 + c), 8, stride=8), :] = f[
                            at : at + 8, 128 * ri : 128 * ri + 128
                        ]
        return 0

    lax.fori_loop(0, 8, rowwise, 0, unroll=True)


def spectrum_kernel(
    start_ref, crop_ref, x_hbm, send_ref, keep_ref, later_ref, row_hi, row_lo, xbuf, table, sums, sem
):
    core = lax.axis_index("core")
    start, crop, row0 = start_ref[0], crop_ref[0], (lax.axis_index("half") * 2 + core) * 128
    copies = []
    for o in range(2):
        for h, chunk in enumerate(CHUNKS[o]):
            rows = pl.ds(*chunk)
            cp = pltpu.make_async_copy(x_hbm.at[rows, o], xbuf.at[o, rows], sem.at[o, h])
            cp.start()
            copies.append(cp)

    scale = 1.0 / math.sqrt(NT)

    lane = lax.broadcasted_iota(jnp.int32, (1, 128), 1)
    real, first = lane < 64, (lane & 32) == 0
    owner = jnp.where((lane & 16) == 0, 1 - core, core)
    for g, (residues, sign) in enumerate(GROUPS):
        kappa = (jnp.where(first, residues[0], residues[1]) - start) & 7
        freq = start + kappa + 8 * ((lane & 8) * 2 + owner * 8 + (lane & 7))

        def one_table(i, _, g=g, sign=sign, freq=freq):
            t = i * 64 + lax.broadcasted_iota(jnp.int32, (64, 128), 0)
            cos, sin = cos_sin((freq * t) & (TURN - 1))
            cos, sin = cos * scale, sin * scale
            a = jnp.where(real, cos, -sin)
            if sign == 0:
                a, b = jnp.where(first, a, 0.0), jnp.where(first, 0.0, a)
            else:
                b = jnp.where(real, sin, cos) * jnp.where(first, float(sign), float(-sign))
            for at, val in ((0, a), (FOLD, b)):
                hi, lo = split(val)
                rows = pl.ds(pl.multiple_of(at + i * 64, 64), 64)
                table[g, rows, 0:128] = hi
                table[g, rows, 128:256] = lo
            return 0

        lax.fori_loop(0, FOLD // 64, one_table, 0)

    rscale = 1.0 / math.sqrt(NR)
    r = row0 + lax.broadcasted_iota(jnp.int32, (128, CROP), 0)
    p = crop + lax.broadcasted_iota(jnp.int32, (128, CROP), 1)
    cos, sin = cos_sin(((r * p) & (NR - 1)) * (TURN // NR))
    cos, sin = cos * rscale, sin * rscale
    for rows, cols, val in ((0, 0, cos), (0, 128, -sin), (128, 0, sin), (128, 128, cos)):
        hi, lo = split(val)
        row_hi[rows : rows + 128, cols : cols + 128] = hi
        row_lo[rows : rows + 128, cols : cols + 128] = lo

    for o, spectra in ((0, sums), (1, later_ref)):
        for h, (first, count) in enumerate(CHUNKS[o]):
            copies[3 * o + h].wait()
            pixels = xbuf.at[o].reshape(1024, NT)

            def delays(i, _, first=first, pixels=pixels, spectra=spectra):
                rows = pl.ds(pl.multiple_of(first * 8 + i * 256, 256), 256)
                inputs = folded([pixels[rows, FOLD * j : FOLD * (j + 1)] for j in range(8)])
                for g in range(4):
                    hi, lo = split(jnp.concatenate(inputs[g], axis=1))
                    d = dot(hi, table[g], NN_DIMS) + dot(lo, table[g], NN_DIMS)
                    spectra[g, rows, :] = d[:, 0:128] + d[:, 128:256]
                return 0

            lax.fori_loop(0, count // 32, delays, 0, unroll=True)
        if o == 0:
            row_stage(start, sums, row_hi, row_lo, send_ref, keep_ref)


VMEM = pl.BlockSpec(memory_space=pltpu.VMEM)
SMEM = pl.BlockSpec(memory_space=pltpu.SMEM)
OCTET = jax.ShapeDtypeStruct((2048, 128), F32)


def spectrum_call(start, crop, x):
    return pl.pallas_call(
        spectrum_kernel,
        out_shape=(
            OCTET,
            OCTET,
            jax.ShapeDtypeStruct((4, 1024, 128), F32),
            jax.ShapeDtypeStruct((256, 256), BF16),
            jax.ShapeDtypeStruct((256, 256), BF16),
        ),
        in_specs=[SMEM, SMEM, pl.BlockSpec(memory_space=pl.ANY)],
        out_specs=(VMEM,) * 5,
        scratch_shapes=[
            pltpu.VMEM((2, 128, 8, NT), F32),
            pltpu.VMEM((4, 2 * FOLD, 256), BF16),
            pltpu.VMEM((4, 1024, 128), F32),
            pltpu.SemaphoreType.DMA((2, 3)),
        ],
        compiler_params=pltpu.CompilerParams(vmem_limit_bytes=40 * 2**20),
        name="spectrum",
    )(start, crop, x.reshape(128, 2, 8, NT))


def row_kernel(start_ref, sums, row_hi, row_lo, send_ref, keep_ref):
    row_stage(start_ref[0], sums, row_hi, row_lo, send_ref, keep_ref)


def row_call(start, sums, row_hi, row_lo):
    return pl.pallas_call(
        row_kernel,
        out_shape=(OCTET, OCTET),
        in_specs=[SMEM, VMEM, VMEM, VMEM],
        out_specs=(VMEM, VMEM),
        cost_estimate=pl.CostEstimate(flops=800_000_000, bytes_accessed=4_000_000, transcendentals=0),
        compiler_params=pltpu.CompilerParams(vmem_limit_bytes=16 * 2**20),
        name="rows",
    )(start, sums, row_hi, row_lo)


def assemble_kernel(keep0, got0, keep1, got1, out_ref):
    for o, (a, b) in enumerate(((keep0, got0), (keep1, got1))):
        for y in range(2):
            for sub in range(4):
                out_ref[y, :, :, sub, o] = (a[y, sub] + b[y, sub]).transpose(1, 0, 2, 3)


def assemble_call(*parts):
    return pl.pallas_call(
        assemble_kernel,
        out_shape=jax.ShapeDtypeStruct((2, 8, 4, 4, 2, 8, 128), F32),
        in_specs=[VMEM] * 4,
        out_specs=VMEM,
        compiler_params=pltpu.CompilerParams(vmem_limit_bytes=8 * 2**20),
        name="assemble",
    )(*(p.reshape(2, 4, 4, 8, 8, 128) for p in parts))


def table_kernel(crop_ref, after_ref, hi_ref, lo_ref):
    del after_ref
    scale = 1.0 / math.sqrt(NC)
    c = lax.broadcasted_iota(jnp.int32, (NC, CROP), 0)
    q = crop_ref[1] + lax.broadcasted_iota(jnp.int32, (NC, CROP), 1)
    cos, sin = cos_sin(((c * q) & (NC - 1)) * (TURN // NC))
    for lane, val in ((0, cos * scale), (128, sin * scale)):
        hi, lo = split(val)
        hi_ref[:, lane : lane + 128] = hi
        lo_ref[:, lane : lane + 128] = lo


def table_call(crop, after):
    out = jax.ShapeDtypeStruct((NC, 256), BF16)
    return pl.pallas_call(
        table_kernel,
        out_shape=(out, out),
        in_specs=[SMEM, pl.BlockSpec(memory_space=pl.ANY)],
        out_specs=(pl.BlockSpec(memory_space=pltpu.VMEM),) * 2,
        cost_estimate=pl.CostEstimate(flops=4_000_000, bytes_accessed=4_000_000, transcendentals=0),
        compiler_params=pltpu.CompilerParams(vmem_limit_bytes=8 * 2**20),
        name="table",
    )(crop, after)


def focal_kernel(hi_ref, lo_ref, g_ref, out_ref):
    for e in range(2):
        g = [(g_ref[0:32, 2 * e + ri] + g_ref[32:64, 2 * e + ri]).reshape(NC, CROP) for ri in range(2)]
        u = dot3(split(jnp.concatenate(g, axis=1)), (hi_ref[...], lo_ref[...]), TN_DIMS)
        out_ref[0, e] = u[0:128, 0:128] + u[128:256, 128:256]
        out_ref[1, e] = u[128:256, 0:128] - u[0:128, 128:256]


def focal_call(table, g):
    return pl.pallas_call(
        focal_kernel,
        out_shape=jax.ShapeDtypeStruct((2, 2, CROP, CROP), F32),
        in_specs=[VMEM] * 3,
        out_specs=VMEM,
        compiler_params=pltpu.CompilerParams(vmem_limit_bytes=16 * 2**20),
        name="focal",
    )(*table, g)


def on_device(interferogram, sideband_start, crop_start):
    cores = [(0, 1), (1, 0)]
    send0, keep0, later, *row_table = spectrum_call(sideband_start, crop_start, interferogram)
    got0 = lax.ppermute(send0, "core", cores)
    send1, keep1 = row_call(sideband_start, later, *row_table)
    got1 = lax.ppermute(send1, "core", cores)
    got1, table = lax.optimization_barrier((got1, table_call(crop_start, got0)))
    mine = assemble_call(keep0, got0, keep1, got1).reshape(64, 64, 128)
    gathered = lax.all_to_all(mine, ("half", "col"), split_axis=0, concat_axis=0, tiled=True)
    return focal_call(table, gathered.reshape(64, 4, 16, 128))


def solution(mesh):
    mesh = Mesh(mesh.devices.reshape(2, 2, 32), ("half", "core", "col"))
    return jax.shard_map(
        on_device,
        mesh=mesh,
        in_specs=(P(("half", "core"), "col", None), P(), P()),
        out_specs=P(None, ("half", "core", "col"), None, None),
        check_vma=False,
    )
```

```python
import functools
import math

import jax
import jax.numpy as jnp
from jax import lax
from jax.experimental import pallas as pl
from jax.experimental.pallas import tpu as pltpu
from jax.sharding import Mesh
from jax.sharding import PartitionSpec as P

NR = 512
NC = 512
NT = 2048
NB = 256
CROP = 128
TURN = 2048
F32 = jnp.float32
BF16 = jnp.bfloat16


def cos_sin(u):
    v = u + 256
    quadrant = (v >> 9) & 3
    r = ((v & 511) - 256).astype(F32) * (2.0 * math.pi / TURN)
    z = r * r
    s = r + r * z * (-1.6666654611e-1 + z * (8.3321608736e-3 + z * -1.9515295891e-4))
    c = 1.0 - 0.5 * z + z * z * (4.166664568298827e-2 + z * (-1.388731625493765e-3 + z * 2.443315711809948e-5))
    odd = (quadrant & 1) == 1
    cos = jnp.where(odd, s, c)
    sin = jnp.where(odd, c, s)
    cos = jnp.where((quadrant == 1) | (quadrant == 2), -cos, cos)
    sin = jnp.where(quadrant >= 2, -sin, sin)
    return cos, sin


def split(a):
    hi = a.astype(BF16)
    return hi, (a - hi.astype(F32)).astype(BF16)


def dot(a, b, dims):
    return lax.dot_general(a, b, (dims, ((), ())), preferred_element_type=F32)


def dot3(a, b, dims):
    return dot(a[0], b[0], dims) + (dot(a[0], b[1], dims) + dot(a[1], b[0], dims))


NN_DIMS = ((1,), (0,))
TN_DIMS = ((0,), (0,))


CHUNKS = (((0, 32), (32, 32), (64, 64)), ((0, 64), (64, 32), (96, 32)))
FOLD = NT // 8
GROUPS = (((0, 4), 0), ((2, 6), -1), ((1, 7), -1), ((3, 5), 1))


def folded(x):
    s = [x[j] + x[j + 4] for j in range(4)]
    d = [x[j] - x[j + 4] for j in range(4)]
    p, q = s[0] + s[2], s[1] + s[3]
    u, v = (d[1] - d[3]) * math.sqrt(0.5), (d[1] + d[3]) * math.sqrt(0.5)
    return ((p + q, p - q), (s[0] - s[2], s[1] - s[3]), (d[0] + u, d[2] + v), (d[0] - u, d[2] - v))


def row_stage(start, sums, row_hi, row_lo, send_ref, keep_ref):
    base = []
    for residues, _ in GROUPS:
        for residue in residues:
            kappa = (residue - start) & 7
            base.append((kappa >> 1) * 64 + (kappa & 1) * 512)

    def rowwise(c, _):
        blocks = []
        for g in range(4):
            s = sums[g, pl.ds(c, 128, stride=8), :].T
            blocks.append(jnp.concatenate([s[0:64], s[64:128]], axis=1))
        f = dot3(split(jnp.concatenate(blocks, axis=0)), (row_hi[...], row_lo[...]), NN_DIMS)
        for n in range(8):
            for rel, ref in ((0, send_ref), (1, keep_ref)):
                for y in range(2):
                    at = n * 32 + rel * 16 + y * 8
                    for ri in range(2):
                        ref[pl.ds(base[n] + (y * 1024 + ri * 256 + c), 8, stride=8), :] = f[
                            at : at + 8, 128 * ri : 128 * ri + 128
                        ]
        return 0

    lax.fori_loop(0, 8, rowwise, 0, unroll=True)


def spectrum_kernel(start_ref, x_hbm, first_ref, second_ref, xbuf, table, sem):
    core, start = lax.axis_index("core"), start_ref[0]
    copies = []
    for o in range(2):
        for h, chunk in enumerate(CHUNKS[o]):
            rows = pl.ds(*chunk)
            cp = pltpu.make_async_copy(x_hbm.at[rows, o], xbuf.at[o, rows], sem.at[o, h])
            cp.start()
            copies.append(cp)

    scale = 1.0 / math.sqrt(NT)

    lane = lax.broadcasted_iota(jnp.int32, (1, 128), 1)
    real, first = lane < 64, (lane & 32) == 0
    owner = jnp.where((lane & 16) == 0, 1 - core, core)
    for g, (residues, sign) in enumerate(GROUPS):
        kappa = (jnp.where(first, residues[0], residues[1]) - start) & 7
        freq = start + kappa + 8 * ((lane & 8) * 2 + owner * 8 + (lane & 7))

        def one_table(i, _, g=g, sign=sign, freq=freq):
            t = i * 64 + lax.broadcasted_iota(jnp.int32, (64, 128), 0)
            cos, sin = cos_sin((freq * t) & (TURN - 1))
            cos, sin = cos * scale, sin * scale
            a = jnp.where(real, cos, -sin)
            if sign == 0:
                a, b = jnp.where(first, a, 0.0), jnp.where(first, 0.0, a)
            else:
                b = jnp.where(real, sin, cos) * jnp.where(first, float(sign), float(-sign))
            for at, val in ((0, a), (FOLD, b)):
                hi, lo = split(val)
                rows = pl.ds(pl.multiple_of(at + i * 64, 64), 64)
                table[g, rows, 0:128] = hi
                table[g, rows, 128:256] = lo
            return 0

        lax.fori_loop(0, FOLD // 64, one_table, 0)

    for o, spectra in ((0, first_ref), (1, second_ref)):
        for h, (first, count) in enumerate(CHUNKS[o]):
            copies[3 * o + h].wait()
            pixels = xbuf.at[o].reshape(1024, NT)

            def delays(i, _, first=first, pixels=pixels, spectra=spectra):
                rows = pl.ds(pl.multiple_of(first * 8 + i * 256, 256), 256)
                inputs = folded([pixels[rows, FOLD * j : FOLD * (j + 1)] for j in range(8)])
                for g in range(4):
                    hi, lo = split(jnp.concatenate(inputs[g], axis=1))
                    d = dot(jnp.concatenate([hi, lo], axis=0), table[g], NN_DIMS)
                    d = d[0:256] + d[256:512]
                    spectra[g, rows, :] = d[:, 0:128] + d[:, 128:256]
                return 0

            lax.fori_loop(0, count // 32, delays, 0, unroll=True)


VMEM = pl.BlockSpec(memory_space=pltpu.VMEM)
SMEM = pl.BlockSpec(memory_space=pltpu.SMEM)
OCTET = jax.ShapeDtypeStruct((2048, 128), F32)
ROW_TABLE = jax.ShapeDtypeStruct((256, 256), BF16)


def spectrum_call(start, x):
    return pl.pallas_call(
        spectrum_kernel,
        out_shape=(jax.ShapeDtypeStruct((4, 1024, 128), F32),) * 2,
        in_specs=[SMEM, pl.BlockSpec(memory_space=pl.ANY)],
        out_specs=(VMEM, VMEM),
        scratch_shapes=[
            pltpu.VMEM((2, 128, 8, NT), F32),
            pltpu.VMEM((4, 2 * FOLD, 256), BF16),
            pltpu.SemaphoreType.DMA((2, 3)),
        ],
        compiler_params=pltpu.CompilerParams(vmem_limit_bytes=40 * 2**20),
        name="spectrum",
    )(start, x.reshape(128, 2, 8, NT))


def first_rows_kernel(start_ref, crop_ref, sums, send_ref, keep_ref, row_hi, row_lo):
    crop, row0 = crop_ref[0:1, 0:1], (lax.axis_index("half") * 2 + lax.axis_index("core")) * 128
    rscale = 1.0 / math.sqrt(NR)
    r = row0 + lax.broadcasted_iota(jnp.int32, (128, CROP), 0)
    p = crop + lax.broadcasted_iota(jnp.int32, (128, CROP), 1)
    cos, sin = cos_sin(((r * p) & (NR - 1)) * (TURN // NR))
    cos, sin = cos * rscale, sin * rscale
    for rows, cols, val in ((0, 0, cos), (0, 128, -sin), (128, 0, sin), (128, 128, cos)):
        hi, lo = split(val)
        row_hi[rows : rows + 128, cols : cols + 128] = hi
        row_lo[rows : rows + 128, cols : cols + 128] = lo
    row_stage(start_ref[0], sums, row_hi, row_lo, send_ref, keep_ref)


def first_rows_call(start, crop, sums):
    return pl.pallas_call(
        first_rows_kernel,
        out_shape=(OCTET, OCTET, ROW_TABLE, ROW_TABLE),
        in_specs=[SMEM, VMEM, VMEM],
        out_specs=(VMEM,) * 4,
        compiler_params=pltpu.CompilerParams(vmem_limit_bytes=16 * 2**20),
        name="first_rows",
    )(start, crop, sums)


def second_rows_kernel(start_ref, sums, row_hi, row_lo, send_ref, keep_ref):
    row_stage(start_ref[0], sums, row_hi, row_lo, send_ref, keep_ref)


def second_rows_call(start, sums, row_hi, row_lo):
    return pl.pallas_call(
        second_rows_kernel,
        out_shape=(OCTET, OCTET),
        in_specs=[SMEM, VMEM, VMEM, VMEM],
        out_specs=(VMEM, VMEM),
        cost_estimate=pl.CostEstimate(flops=800_000_000, bytes_accessed=4_000_000, transcendentals=0),
        compiler_params=pltpu.CompilerParams(vmem_limit_bytes=16 * 2**20),
        name="second_rows",
    )(start, sums, row_hi, row_lo)


def assemble_kernel(keep0, got0, keep1, got1, out_ref):
    for o, (a, b) in enumerate(((keep0, got0), (keep1, got1))):
        for y in range(2):
            for sub in range(4):
                out_ref[y, :, :, sub, o] = (a[y, sub] + b[y, sub]).transpose(1, 0, 2, 3)


def assemble_call(*parts):
    return pl.pallas_call(
        assemble_kernel,
        out_shape=jax.ShapeDtypeStruct((2, 8, 4, 4, 2, 8, 128), F32),
        in_specs=[VMEM] * 4,
        out_specs=VMEM,
        compiler_params=pltpu.CompilerParams(vmem_limit_bytes=8 * 2**20),
        name="assemble",
    )(*(p.reshape(2, 4, 4, 8, 8, 128) for p in parts))


def table_kernel(crop_ref, after_ref, hi_ref, lo_ref):
    del after_ref
    scale = 1.0 / math.sqrt(NC)
    c = lax.broadcasted_iota(jnp.int32, (NC, CROP), 0)
    q = crop_ref[0:1, 1:2] + lax.broadcasted_iota(jnp.int32, (NC, CROP), 1)
    cos, sin = cos_sin(((c * q) & (NC - 1)) * (TURN // NC))
    for lane, val in ((0, cos * scale), (128, sin * scale)):
        hi, lo = split(val)
        hi_ref[:, lane : lane + 128] = hi
        lo_ref[:, lane : lane + 128] = lo


def table_call(crop, after):
    out = jax.ShapeDtypeStruct((NC, 256), BF16)
    return pl.pallas_call(
        table_kernel,
        out_shape=(out, out),
        in_specs=[VMEM, pl.BlockSpec(memory_space=pl.ANY)],
        out_specs=(VMEM,) * 2,
        cost_estimate=pl.CostEstimate(flops=4_000_000, bytes_accessed=4_000_000, transcendentals=0),
        compiler_params=pltpu.CompilerParams(vmem_limit_bytes=8 * 2**20),
        name="table",
    )(crop, after)


def focal_kernel(hi_ref, lo_ref, g_ref, out_ref):
    for e in range(2):
        g = [(g_ref[0:32, 2 * e + ri] + g_ref[32:64, 2 * e + ri]).reshape(NC, CROP) for ri in range(2)]
        u = dot3(split(jnp.concatenate(g, axis=1)), (hi_ref[...], lo_ref[...]), TN_DIMS)
        out_ref[0, e] = u[0:128, 0:128] + u[128:256, 128:256]
        out_ref[1, e] = u[128:256, 0:128] - u[0:128, 128:256]


def focal_call(table, g):
    return pl.pallas_call(
        focal_kernel,
        out_shape=jax.ShapeDtypeStruct((2, 2, CROP, CROP), F32),
        in_specs=[VMEM] * 3,
        out_specs=VMEM,
        compiler_params=pltpu.CompilerParams(vmem_limit_bytes=16 * 2**20),
        name="focal",
    )(*table, g)


def on_device(interferogram, sideband_start, crop_start):
    cores = [(0, 1), (1, 0)]
    crop_start = crop_start.reshape(1, 2)
    first, second = spectrum_call(sideband_start, interferogram)
    send0, keep0, *row_table = first_rows_call(sideband_start, crop_start, first)
    got0 = lax.ppermute(send0, "core", cores)
    send1, keep1 = second_rows_call(sideband_start, second, *row_table)
    got1 = lax.ppermute(send1, "core", cores)
    got1, table = lax.optimization_barrier((got1, table_call(crop_start, got0)))
    mine = assemble_call(keep0, got0, keep1, got1).reshape(64, 64, 128)
    gathered = lax.all_to_all(mine, ("half", "col"), split_axis=0, concat_axis=0, tiled=True)
    return focal_call(table, gathered.reshape(64, 4, 16, 128))


def solution(mesh):
    mesh = Mesh(mesh.devices.reshape(2, 2, 32), ("half", "core", "col"))
    return jax.shard_map(
        on_device,
        mesh=mesh,
        in_specs=(P(("half", "core"), "col", None), P(), P()),
        out_specs=P(None, ("half", "core", "col"), None, None),
        check_vma=False,
    )
```

```python
import functools
import math

import jax
import jax.numpy as jnp
from jax import lax
from jax.experimental import pallas as pl
from jax.experimental.pallas import tpu as pltpu
from jax.sharding import Mesh
from jax.sharding import PartitionSpec as P

NR = 512
NC = 512
NT = 2048
NB = 256
CROP = 128
TURN = 2048
F32 = jnp.float32
BF16 = jnp.bfloat16


def cos_sin(u):
    v = u + 256
    quadrant = (v >> 9) & 3
    r = ((v & 511) - 256).astype(F32) * (2.0 * math.pi / TURN)
    z = r * r
    s = r + r * z * (-1.6666654611e-1 + z * (8.3321608736e-3 + z * -1.9515295891e-4))
    c = 1.0 - 0.5 * z + z * z * (4.166664568298827e-2 + z * (-1.388731625493765e-3 + z * 2.443315711809948e-5))
    odd = (quadrant & 1) == 1
    cos = jnp.where(odd, s, c)
    sin = jnp.where(odd, c, s)
    cos = jnp.where((quadrant == 1) | (quadrant == 2), -cos, cos)
    sin = jnp.where(quadrant >= 2, -sin, sin)
    return cos, sin


def split(a):
    hi = a.astype(BF16)
    return hi, (a - hi.astype(F32)).astype(BF16)


def dot(a, b, dims):
    return lax.dot_general(a, b, (dims, ((), ())), preferred_element_type=F32)


def dot3(a, b, dims):
    at = dims[0][0]
    return dot(jnp.concatenate([a[0], a[0], a[1]], axis=at), jnp.concatenate([b[0], b[1], b[0]], axis=0), dims)


NN_DIMS = ((1,), (0,))
TN_DIMS = ((0,), (0,))


CHUNKS = (((0, 32), (32, 32), (64, 64)), ((0, 64), (64, 32), (96, 32)))
FOLD = NT // 8
GROUPS = (((0, 4), 0), ((2, 6), -1), ((1, 7), -1), ((3, 5), 1))


def folded(x):
    s = [x[j] + x[j + 4] for j in range(4)]
    d = [x[j] - x[j + 4] for j in range(4)]
    p, q = s[0] + s[2], s[1] + s[3]
    u, v = (d[1] - d[3]) * math.sqrt(0.5), (d[1] + d[3]) * math.sqrt(0.5)
    return ((p + q, p - q), (s[0] - s[2], s[1] - s[3]), (d[0] + u, d[2] + v), (d[0] - u, d[2] - v))


def row_stage(start, sums, row_hi, row_lo, send_ref, keep_ref):
    base = []
    for residues, _ in GROUPS:
        for residue in residues:
            kappa = (residue - start) & 7
            base.append((kappa >> 1) * 64 + (kappa & 1) * 512)

    def rowwise(c, _):
        blocks = []
        for g in range(4):
            s = sums[g, pl.ds(c, 128, stride=8), :].T
            blocks.append(jnp.concatenate([s[0:64], s[64:128]], axis=1))
        f = dot3(split(jnp.concatenate(blocks, axis=0)), (row_hi[...], row_lo[...]), NN_DIMS)
        for n in range(8):
            for rel, ref in ((0, send_ref), (1, keep_ref)):
                for y in range(2):
                    at = n * 32 + rel * 16 + y * 8
                    for ri in range(2):
                        ref[pl.ds(base[n] + (y * 1024 + ri * 256 + c), 8, stride=8), :] = f[
                            at : at + 8, 128 * ri : 128 * ri + 128
                        ]
        return 0

    lax.fori_loop(0, 8, rowwise, 0, unroll=True)


def spectrum_kernel(start_ref, x_hbm, first_ref, second_ref, xbuf, table, sem):
    core, start = lax.axis_index("core"), start_ref[0]
    copies = []
    for o in range(2):
        for h, chunk in enumerate(CHUNKS[o]):
            rows = pl.ds(*chunk)
            cp = pltpu.make_async_copy(x_hbm.at[rows, o], xbuf.at[o, rows], sem.at[o, h])
            cp.start()
            copies.append(cp)

    scale = 1.0 / math.sqrt(NT)

    lane = lax.broadcasted_iota(jnp.int32, (1, 128), 1)
    real, first = lane < 64, (lane & 32) == 0
    owner = jnp.where((lane & 16) == 0, 1 - core, core)
    for g, (residues, sign) in enumerate(GROUPS):
        kappa = (jnp.where(first, residues[0], residues[1]) - start) & 7
        freq = start + kappa + 8 * ((lane & 8) * 2 + owner * 8 + (lane & 7))

        def one_table(i, _, g=g, sign=sign, freq=freq):
            t = i * 64 + lax.broadcasted_iota(jnp.int32, (64, 128), 0)
            cos, sin = cos_sin((freq * t) & (TURN - 1))
            cos, sin = cos * scale, sin * scale
            a = jnp.where(real, cos, -sin)
            if sign == 0:
                a, b = jnp.where(first, a, 0.0), jnp.where(first, 0.0, a)
            else:
                b = jnp.where(real, sin, cos) * jnp.where(first, float(sign), float(-sign))
            for at, val in ((0, a), (FOLD, b)):
                hi, lo = split(val)
                rows = pl.ds(pl.multiple_of(at + i * 64, 64), 64)
                table[g, rows, 0:128] = hi
                table[g, rows, 128:256] = lo
            return 0

        lax.fori_loop(0, FOLD // 64, one_table, 0)

    for o, spectra in ((0, first_ref), (1, second_ref)):
        for h, (first, count) in enumerate(CHUNKS[o]):
            copies[3 * o + h].wait()
            pixels = xbuf.at[o].reshape(1024, NT)

            def delays(i, _, first=first, pixels=pixels, spectra=spectra):
                rows = pl.ds(pl.multiple_of(first * 8 + i * 256, 256), 256)
                inputs = folded([pixels[rows, FOLD * j : FOLD * (j + 1)] for j in range(8)])
                for g in range(4):
                    hi, lo = split(jnp.concatenate(inputs[g], axis=1))
                    d = dot(jnp.concatenate([hi, lo], axis=0), table[g], NN_DIMS)
                    d = d[0:256] + d[256:512]
                    spectra[g, rows, :] = d[:, 0:128] + d[:, 128:256]
                return 0

            lax.fori_loop(0, count // 32, delays, 0, unroll=True)


VMEM = pl.BlockSpec(memory_space=pltpu.VMEM)
SMEM = pl.BlockSpec(memory_space=pltpu.SMEM)
OCTET = jax.ShapeDtypeStruct((2048, 128), F32)
ROW_TABLE = jax.ShapeDtypeStruct((256, 256), BF16)


def spectrum_call(start, x):
    return pl.pallas_call(
        spectrum_kernel,
        out_shape=(jax.ShapeDtypeStruct((4, 1024, 128), F32),) * 2,
        in_specs=[SMEM, pl.BlockSpec(memory_space=pl.ANY)],
        out_specs=(VMEM, VMEM),
        scratch_shapes=[
            pltpu.VMEM((2, 128, 8, NT), F32),
            pltpu.VMEM((4, 2 * FOLD, 256), BF16),
            pltpu.SemaphoreType.DMA((2, 3)),
        ],
        compiler_params=pltpu.CompilerParams(vmem_limit_bytes=40 * 2**20),
        name="spectrum",
    )(start, x.reshape(128, 2, 8, NT))


def first_rows_kernel(start_ref, crop_ref, sums, send_ref, keep_ref, row_hi, row_lo):
    crop, row0 = crop_ref[0:1, 0:1], (lax.axis_index("half") * 2 + lax.axis_index("core")) * 128
    rscale = 1.0 / math.sqrt(NR)
    r = row0 + lax.broadcasted_iota(jnp.int32, (128, CROP), 0)
    p = crop + lax.broadcasted_iota(jnp.int32, (128, CROP), 1)
    cos, sin = cos_sin(((r * p) & (NR - 1)) * (TURN // NR))
    cos, sin = cos * rscale, sin * rscale
    for table, c, s in zip((row_hi, row_lo), split(cos), split(sin)):
        table[0:128, 0:128] = c
        table[0:128, 128:256] = -s
        table[128:256, 0:128] = s
        table[128:256, 128:256] = c
    row_stage(start_ref[0], sums, row_hi, row_lo, send_ref, keep_ref)


def first_rows_call(start, crop, sums):
    return pl.pallas_call(
        first_rows_kernel,
        out_shape=(OCTET, OCTET, ROW_TABLE, ROW_TABLE),
        in_specs=[SMEM, VMEM, VMEM],
        out_specs=(VMEM,) * 4,
        compiler_params=pltpu.CompilerParams(vmem_limit_bytes=16 * 2**20),
        name="first_rows",
    )(start, crop, sums)


def second_rows_kernel(start_ref, sums, row_hi, row_lo, send_ref, keep_ref):
    row_stage(start_ref[0], sums, row_hi, row_lo, send_ref, keep_ref)


def second_rows_call(start, sums, row_hi, row_lo):
    return pl.pallas_call(
        second_rows_kernel,
        out_shape=(OCTET, OCTET),
        in_specs=[SMEM, VMEM, VMEM, VMEM],
        out_specs=(VMEM, VMEM),
        cost_estimate=pl.CostEstimate(flops=800_000_000, bytes_accessed=4_000_000, transcendentals=0),
        compiler_params=pltpu.CompilerParams(vmem_limit_bytes=16 * 2**20),
        name="second_rows",
    )(start, sums, row_hi, row_lo)


def assemble_kernel(keep0, got0, keep1, got1, out_ref):
    for o, (a, b) in enumerate(((keep0, got0), (keep1, got1))):
        for y in range(2):
            for sub in range(4):
                out_ref[y, :, :, sub, o] = (a[y, sub] + b[y, sub]).transpose(1, 0, 2, 3)


def assemble_call(*parts):
    return pl.pallas_call(
        assemble_kernel,
        out_shape=jax.ShapeDtypeStruct((2, 8, 4, 4, 2, 8, 128), F32),
        in_specs=[VMEM] * 4,
        out_specs=VMEM,
        compiler_params=pltpu.CompilerParams(vmem_limit_bytes=8 * 2**20),
        name="assemble",
    )(*(p.reshape(2, 4, 4, 8, 8, 128) for p in parts))


def table_kernel(crop_ref, after_ref, hi_ref, lo_ref):
    del after_ref
    scale = 1.0 / math.sqrt(NC)
    c = lax.broadcasted_iota(jnp.int32, (NC, CROP), 0)
    q = crop_ref[0:1, 1:2] + lax.broadcasted_iota(jnp.int32, (NC, CROP), 1)
    cos, sin = cos_sin(((c * q) & (NC - 1)) * (TURN // NC))
    for lane, val in ((0, cos * scale), (128, sin * scale)):
        hi, lo = split(val)
        hi_ref[:, lane : lane + 128] = hi
        lo_ref[:, lane : lane + 128] = lo


def table_call(crop, after):
    out = jax.ShapeDtypeStruct((NC, 256), BF16)
    return pl.pallas_call(
        table_kernel,
        out_shape=(out, out),
        in_specs=[VMEM, pl.BlockSpec(memory_space=pl.ANY)],
        out_specs=(VMEM,) * 2,
        cost_estimate=pl.CostEstimate(flops=4_000_000, bytes_accessed=4_000_000, transcendentals=0),
        compiler_params=pltpu.CompilerParams(vmem_limit_bytes=8 * 2**20),
        name="table",
    )(crop, after)


def focal_kernel(hi_ref, lo_ref, g_ref, out_ref):
    for e in range(2):
        g = [(g_ref[0:32, 2 * e + ri] + g_ref[32:64, 2 * e + ri]).reshape(NC, CROP) for ri in range(2)]
        u = dot3(split(jnp.concatenate(g, axis=1)), (hi_ref[...], lo_ref[...]), TN_DIMS)
        out_ref[0, e] = u[0:128, 0:128] + u[128:256, 128:256]
        out_ref[1, e] = u[128:256, 0:128] - u[0:128, 128:256]


def focal_call(table, g):
    return pl.pallas_call(
        focal_kernel,
        out_shape=jax.ShapeDtypeStruct((2, 2, CROP, CROP), F32),
        in_specs=[VMEM] * 3,
        out_specs=VMEM,
        compiler_params=pltpu.CompilerParams(vmem_limit_bytes=16 * 2**20),
        name="focal",
    )(*table, g)


def on_device(interferogram, sideband_start, crop_start):
    cores = [(0, 1), (1, 0)]
    crop_start = crop_start.reshape(1, 2)
    first, second = spectrum_call(sideband_start, interferogram)
    send0, keep0, *row_table = first_rows_call(sideband_start, crop_start, first)
    got0 = lax.ppermute(send0, "core", cores)
    send1, keep1 = second_rows_call(sideband_start, second, *row_table)
    got1 = lax.ppermute(send1, "core", cores)
    got1, table = lax.optimization_barrier((got1, table_call(crop_start, got0)))
    mine = assemble_call(keep0, got0, keep1, got1).reshape(64, 64, 128)
    gathered = lax.all_to_all(mine, ("half", "col"), split_axis=0, concat_axis=0, tiled=True)
    return focal_call(table, gathered.reshape(64, 4, 16, 128))


def solution(mesh):
    mesh = Mesh(mesh.devices.reshape(2, 2, 32), ("half", "core", "col"))
    return jax.shard_map(
        on_device,
        mesh=mesh,
        in_specs=(P(("half", "core"), "col", None), P(), P()),
        out_specs=P(None, ("half", "core", "col"), None, None),
        check_vma=False,
    )
```
